32 devices in a mesh: groups: 2 (over x), seq: 16 (over z, y, core).
Axes of the slice: x: 2, y: 2, z: 4, core: 2. Of those that a mesh axis runs over, the one named last changes fastest.
Arguments:
- qkv: bfloat16 [4096, 9216], P(('groups', 'seq')), parts along dimension 0, may hold values from -8 to 8, as said below
- output_gradient: bfloat16 [4096, 3072], P(('groups', 'seq')), parts along dimension 0, may hold values from -6 to 6
- adapter_down_weight: bfloat16 [3072, 64], replicated, may hold values from -0.109375 to 0.109375
- adapter_up_weight: bfloat16 [64, 3072], replicated, may hold values from -0.75 to 0.75
- listed_key_blocks: int32 [48, 16, 10], replicated, may hold values from 0 to 15
- key_block_count: int32 [48], replicated, may hold values from 1 to 10
Outputs:
- grad_qkv: bfloat16 [4096, 9216], P(('groups', 'seq')), parts along dimension 0
- grad_down: float32 [6144, 64], P('groups'), parts along dimension 0
- grad_up: float32 [128, 3072], P('groups'), parts along dimension 0
The draws below stay inside these ranges and needn't reach their ends.
There are 2 independent parts, one for each index of `groups`. The reference program is written for one: setup_inputs(seed, part) draws one part's arguments, and reference() takes and returns one part's arrays. A program takes and returns all parts, laid end to end along the dimension named above; an argument that names none is the same for every part. Nothing has to cross between parts.
Inputs may be any that keep to these rules, and one draw needn't show every extreme that they name: `qkv`: query, key and value entries.
All inputs are finite; a program needn't handle non-finite values.
Results may differ from the reference program's by a relative error of at most 0.019.
Values may be sent and summed in bfloat16 or wider, within the bound.
A program may use at most 192 MiB of HBM per device.

```python
import jax
import jax.numpy as jnp
from jax import lax

MODEL_WIDTH = 3072
H = 48
E = 64
ADAPTER_RANK = 64
BLOCK = 128
KB = 10
ITEMS_DEV = 3
TOK_DEV = 128
TOKENS = 2048
QSEG = 1


def draw_qkv(key, part):
    key = jax.random.fold_in(key, 11)
    base_key = jax.random.fold_in(key, 0)
    values = jax.random.truncated_normal(base_key, -4.0, 4.0, (TOKENS, 3, H, E), jnp.float32)
    return values.reshape(TOKENS, 3 * H * E).astype(jnp.bfloat16)


def draw_listed_key_blocks(key, part):
    key = jax.random.fold_in(key, 23)
    kind_key, stride_key, column_key = jax.random.split(key, 3)
    block_total = TOKENS // BLOCK
    pattern = jax.random.randint(kind_key, (H, 1, 1), 0, 3)
    strides = jax.random.randint(stride_key, (H, 1, 1), 2, max(3, block_total // KB))
    columns = jax.random.randint(column_key, (H, 1, KB), 0, block_total)
    row_ids = jnp.arange(block_total, dtype=jnp.int32)[None, :, None]
    slot_pos = jnp.arange(KB, dtype=jnp.int32)[None, None, :]
    distance = (slot_pos + 1) // 2
    direction = jnp.where(slot_pos % 2 == 1, 1, -1)
    banded = (row_ids + direction * distance) % block_total
    diagonal = (row_ids + direction * distance * strides) % block_total
    barred = jnp.broadcast_to(columns, (H, block_total, KB))
    picked = jnp.where(pattern == 0, banded, jnp.where(pattern == 1, diagonal, barred))
    picked = jnp.where(slot_pos == 0, row_ids, picked)
    return picked.astype(jnp.int32)


def draw_key_block_count(key, part):
    key = jax.random.fold_in(key, 31)
    dense_key, level_key, fullest_key, sparsest_key = jax.random.split(key, 4)
    dense = jax.random.randint(dense_key, (H,), 0, 4) == 0
    counts = jnp.where(dense, KB, 2 + jax.random.randint(level_key, (H,), 0, max(1, KB // 2 - 1)))
    fullest = jax.random.randint(fullest_key, (), 0, H)
    sparsest = (fullest + 1 + jax.random.randint(sparsest_key, (), 0, H - 1)) % H
    counts = counts.at[fullest].set(KB).at[sparsest].set(1)
    return counts.astype(jnp.int32)


def level_of(key, shape, pieces, least, largest):
    loudness = 1.0
    for dim, blocks in pieces:
        steps = jax.random.uniform(jax.random.fold_in(jax.random.fold_in(key, 6), dim), (blocks,), jnp.float32, least / len(pieces), largest / len(pieces))
        loudness = loudness * jnp.repeat(jnp.exp(steps), shape[dim] // blocks).reshape((-1,) + (1,) * (len(shape) - 1 - dim))
    return loudness


def noise(key, extent, scale, limit, pieces=(), kind=jnp.bfloat16):
    drawn = jax.random.normal(key, extent, jnp.float32) * scale
    if len(pieces) > 0:
        drawn = level_of(key, extent, pieces, -0.22, 0.18) * drawn
    return jnp.clip(drawn, min=-limit, max=limit).astype(kind)


def setup_inputs(seed: int = 0, part: int = 0) -> dict:
    keys = jax.random.split(jax.random.key(seed), 7)
    part_keys = jax.random.split(jax.random.fold_in(keys[6], part), 7)
    qkv = draw_qkv(jax.random.fold_in(jax.random.fold_in(keys[6], part), 71), part)
    output_gradient = noise(part_keys[1], (TOKENS, MODEL_WIDTH), 1.0, 6.0, ((0, 16),))
    adapter_down_weight = noise(keys[2], (MODEL_WIDTH, ADAPTER_RANK), MODEL_WIDTH ** -0.5, 0.109375)
    adapter_up_weight = noise(keys[3], (ADAPTER_RANK, MODEL_WIDTH), ADAPTER_RANK ** -0.5, 0.75)
    listed_key_blocks = draw_listed_key_blocks(jax.random.fold_in(keys[6], 71), part)
    key_block_count = draw_key_block_count(jax.random.fold_in(keys[6], 71), part)
    return dict(qkv=qkv, output_gradient=output_gradient, adapter_down_weight=adapter_down_weight, adapter_up_weight=adapter_up_weight, listed_key_blocks=listed_key_blocks, key_block_count=key_block_count)


def block_scores(queries, gathered, live_cols):
    head_width = queries.shape[-1]
    scores = jnp.einsum("qre,qke->qrk", queries.astype(jnp.float32), gathered[..., :head_width].astype(jnp.float32)) * head_width ** -0.5
    return jnp.where(live_cols, scores, -jnp.inf)


def gather_blocks(keyval, blocks):
    block_total = keyval.shape[0] // BLOCK
    stacked = keyval.reshape(block_total, BLOCK, 2 * E)
    return jnp.take(stacked, blocks, axis=0).reshape(block_total, KB * BLOCK, 2 * E)


def forward_head(inputs):
    queries, keyval, blocks, live_count = inputs
    block_total = queries.shape[0] // BLOCK
    live_cols = (jnp.arange(KB * BLOCK) // BLOCK) < live_count
    gathered = gather_blocks(keyval, blocks)
    query_blocks = queries.reshape(block_total, BLOCK, E)
    scores = block_scores(query_blocks, gathered, live_cols)
    row_peak = jnp.max(scores, axis=-1, keepdims=True)
    log_total = row_peak + jnp.log(jnp.sum(jnp.exp(scores - row_peak), axis=-1, keepdims=True))
    weights = lax.optimization_barrier(jnp.exp(scores - log_total).astype(jnp.bfloat16)).astype(jnp.float32)
    attention_output = jnp.einsum("qrk,qke->qre", weights, gathered[..., E:].astype(jnp.float32)).astype(jnp.bfloat16)
    return attention_output.reshape(block_total * BLOCK, E), log_total


def backward_head(inputs):
    queries, keyval, blocks, live_count, attention_output, grad_rows, log_total, head_id = inputs
    block_total = queries.shape[0] // BLOCK
    live_cols = (jnp.arange(KB * BLOCK) // BLOCK) < live_count
    gathered = gather_blocks(keyval, blocks)
    query_blocks = queries.reshape(block_total, BLOCK, E)
    grad_wide = grad_rows.reshape(block_total, BLOCK, E).astype(jnp.float32)
    attended_wide = attention_output.reshape(block_total, BLOCK, E).astype(jnp.float32)
    scores = block_scores(query_blocks, gathered, live_cols)
    weights = lax.optimization_barrier(jnp.exp(scores - log_total).astype(jnp.bfloat16)).astype(jnp.float32)
    value_grad = jnp.einsum("qrk,qre->qke", weights, grad_wide)
    dotted = lax.optimization_barrier(jnp.einsum("qre,qke->qrk", grad_wide, gathered[..., E:].astype(jnp.float32)).astype(jnp.bfloat16)).astype(jnp.float32)
    row_delta = jnp.sum(grad_wide * attended_wide, axis=-1, keepdims=True)
    score_grad = lax.optimization_barrier((weights * (dotted - row_delta)).astype(jnp.bfloat16)).astype(jnp.float32)
    query_grad = (jnp.einsum("qrk,qke->qre", score_grad, gathered[..., :E].astype(jnp.float32)) * E ** -0.5).astype(jnp.bfloat16)
    key_grad = jnp.einsum("qrk,qre->qke", score_grad, query_blocks.astype(jnp.float32)) * E ** -0.5
    partial_value = jnp.concatenate([key_grad, value_grad], axis=-1).reshape(block_total, KB, BLOCK, 2 * E)
    segment = (jnp.arange(block_total, dtype=jnp.int32) // (TOK_DEV // BLOCK)) % QSEG
    owner_dev = (head_id * QSEG + segment) // ITEMS_DEV - (head_id * QSEG) // ITEMS_DEV
    group_sums = jnp.zeros((QSEG // ITEMS_DEV + 2, block_total, BLOCK, 2 * E), jnp.float32)
    group_sums = group_sums.at[owner_dev[:, None], blocks].add(partial_value)
    rounded = lax.optimization_barrier(group_sums.astype(jnp.bfloat16)).astype(jnp.float32)
    keyval_grad = jnp.sum(rounded, axis=0).astype(jnp.bfloat16).reshape(block_total * BLOCK, 2 * E)
    return query_grad.reshape(block_total * BLOCK, E), keyval_grad


def reference(qkv, output_gradient, adapter_down_weight, adapter_up_weight, listed_key_blocks, key_block_count):
    split_heads = jnp.transpose(qkv.reshape(TOKENS, 3, H, E), (1, 2, 0, 3))
    keyval_heads = jnp.concatenate([split_heads[1], split_heads[2]], axis=-1)
    attended_heads, log_totals = lax.map(forward_head, (split_heads[0], keyval_heads, listed_key_blocks, key_block_count))
    attention_output = jnp.transpose(attended_heads, (1, 0, 2)).reshape(TOKENS, H * E)
    adapter_projected = jnp.dot(attention_output, adapter_down_weight, preferred_element_type=jnp.float32).astype(jnp.bfloat16)
    fetched_rows = jnp.dot(output_gradient, adapter_up_weight.T, preferred_element_type=jnp.float32).astype(jnp.bfloat16)
    attention_output_gradient = (output_gradient.astype(jnp.float32) + jnp.dot(fetched_rows, adapter_down_weight.T, preferred_element_type=jnp.float32)).astype(jnp.bfloat16)
    rescale = TOKENS ** -0.5
    grad_down = jnp.dot(attention_output.T, fetched_rows, preferred_element_type=jnp.float32) * rescale
    grad_up = jnp.dot(adapter_projected.T, output_gradient, preferred_element_type=jnp.float32) * rescale
    grad_heads = jnp.transpose(attention_output_gradient.reshape(TOKENS, H, E), (1, 0, 2))
    query_grads, keyval_grads = lax.map(backward_head, (split_heads[0], keyval_heads, listed_key_blocks, key_block_count, attended_heads, grad_heads, log_totals, jnp.arange(H, dtype=jnp.int32)))
    query_rows = jnp.transpose(query_grads, (1, 0, 2)).reshape(TOKENS, H * E)
    keyval_rows = jnp.transpose(keyval_grads, (1, 0, 2))
    key_rows = keyval_rows[..., :E].reshape(TOKENS, H * E)
    value_rows = keyval_rows[..., E:].reshape(TOKENS, H * E)
    grad_qkv = jnp.concatenate([query_rows, key_rows, value_rows], axis=1)
    return grad_qkv, grad_down, grad_up
```

```python
import jax
import jax.numpy as jnp
import numpy as np
from jax import lax
from jax.experimental import pallas as pl
from jax.experimental.pallas import tpu as pltpu
from jax.sharding import PartitionSpec as P

H = 48
E = 64
BLOCK = 128
KB = 10
ITEMS_DEV = 3


def tables(device_total, segments):
    slot_total = -(-ITEMS_DEV // segments)
    head_slots = min(ITEMS_DEV, (ITEMS_DEV + segments - 2) // segments + 1)
    device = np.repeat(np.arange(device_total), ITEMS_DEV)
    within = np.tile(np.arange(ITEMS_DEV), device_total)
    item_id = device * ITEMS_DEV + within
    head_for = np.full((segments, device_total, slot_total), H, np.int32)
    head_for[item_id % segments, device, within // segments] = item_id // segments
    source_for = np.zeros((segments, H), np.int32)
    source_for[item_id % segments, item_id // segments] = within // segments * device_total + device
    item_heads = (item_id // segments).reshape(device_total, ITEMS_DEV).astype(np.int32)
    first_head = np.arange(device_total) * ITEMS_DEV // segments
    last_head = (np.arange(device_total) * ITEMS_DEV + ITEMS_DEV - 1) // segments
    slot_heads = np.minimum(
        first_head[:, None] + np.arange(head_slots)[None, :], last_head[:, None]
    ).astype(np.int32)
    owned_heads = []
    owned_rows = []
    for slot_pos in range(head_slots):
        usable = first_head + slot_pos <= last_head
        owned_heads.append((first_head + slot_pos)[usable])
        owned_rows.append((slot_pos * device_total + np.arange(device_total))[usable])
    owned_heads = np.concatenate(owned_heads)
    owned_rows = np.concatenate(owned_rows)
    ordering = np.argsort(owned_heads, kind="stable")
    sorted_heads = owned_heads[ordering]
    sorted_rows = owned_rows[ordering]
    position = np.arange(sorted_heads.size) - np.searchsorted(sorted_heads, sorted_heads)
    contributors = np.full((H, int(position.max()) + 1), head_slots * device_total, np.int32)
    contributors[sorted_heads, position] = sorted_rows
    return (head_for, source_for, item_heads, slot_heads, contributors)


def spread_rows(features, targets):
    shard_rows = features.shape[0]
    per_head = jnp.transpose(features.reshape(shard_rows, H, E), (1, 0, 2))
    padded = jnp.concatenate([per_head, jnp.zeros((1, shard_rows, E), features.dtype)], axis=0)
    return jnp.take(padded, targets, axis=0).reshape(targets.shape[0], -1)


def collect_heads(received, sources, shard_rows):
    flattened = received.reshape(-1, shard_rows * E)
    picked = jnp.take(flattened, sources, axis=0)
    return jnp.transpose(picked.reshape(H, shard_rows, E), (1, 0, 2)).reshape(shard_rows, H * E)


def place_items(pieces, segment_ids, slot_total, segments):
    per_source = pieces[0].shape[0]
    buffer = jnp.zeros((slot_total, per_source, segments, pieces[0][0].size), jnp.bfloat16)
    anchor = jnp.zeros((), jnp.int32)
    for within in range(len(pieces)):
        update = pieces[within].reshape(1, per_source, 1, -1)
        slot_start = jnp.full((), within // segments, jnp.int32)
        buffer = lax.dynamic_update_slice(
            buffer, update, (slot_start, anchor, segment_ids[within], anchor)
        )
    return buffer.reshape(slot_total, per_source * segments, -1)


def segmented(
    qkv, output_gradient, adapter_down_weight, adapter_up_weight, listed_key_blocks, key_block_count
):
    device_total = lax.axis_size("seq")
    my_index = lax.axis_index("seq")
    shard_rows = qkv.shape[0]
    segments = ITEMS_DEV * device_total // H
    slot_total = -(-ITEMS_DEV // segments)
    per_source = device_total // segments
    blocks_per_shard = shard_rows // BLOCK
    block_total = device_total * blocks_per_shard
    head_for, source_for, item_heads, slot_heads, contributors = tables(device_total, segments)
    head_slots = slot_heads.shape[1]
    residue = my_index % segments
    targets = lax.dynamic_index_in_dim(jnp.asarray(head_for), residue, 0, False)
    sources = lax.dynamic_index_in_dim(jnp.asarray(source_for), residue, 0, False)
    query_send = spread_rows(qkv[:, : H * E], targets)
    key_part = qkv[:, H * E : 2 * H * E].reshape(shard_rows, H, E)
    value_part = qkv[:, 2 * H * E :].reshape(shard_rows, H, E)
    keyval_heads = jnp.transpose(
        jnp.concatenate([key_part, value_part], axis=2), (1, 0, 2)
    ).reshape(H, shard_rows * 2 * E)
    first_head = my_index * ITEMS_DEV // segments
    received_queries, received_keyval = (
        lax.all_to_all(query_send, "seq", split_axis=0, concat_axis=0, tiled=True),
        lax.all_to_all(
            jnp.take(keyval_heads, jnp.asarray(item_heads), axis=0),
            "seq",
            split_axis=0,
            concat_axis=0,
            tiled=True,
        ),
    )
    queries_by_source = received_queries.reshape(per_source, segments, slot_total, shard_rows, E)
    keyval_by_slot = received_keyval.reshape(device_total, -1, shard_rows * 2 * E)
    source_ids = jnp.arange(per_source, dtype=jnp.int32)
    column_block = jnp.arange(KB * BLOCK, dtype=jnp.int32) // BLOCK
    saved = []
    for within in range(ITEMS_DEV):
        item_id = my_index * ITEMS_DEV + within
        item_head = item_id // segments
        segment = item_id % segments
        queries = lax.dynamic_index_in_dim(queries_by_source, segment, 1, False)[
            :, within // segments
        ]
        query_ids = (
            (segment + segments * source_ids)[:, None] * blocks_per_shard
            + jnp.arange(blocks_per_shard, dtype=jnp.int32)[None, :]
        ).reshape(-1)
        item_blocks = jnp.take(
            lax.dynamic_index_in_dim(listed_key_blocks, item_head, 0, False), query_ids, axis=0
        )
        keyval_item = lax.dynamic_index_in_dim(keyval_by_slot, within, 1, False).reshape(
            block_total, BLOCK, 2 * E
        )
        gathered = jnp.take(keyval_item, item_blocks, axis=0).reshape(-1, KB * BLOCK, 2 * E)
        live_cols = column_block < key_block_count[item_head]
        raw_scores = jnp.einsum(
            "qre,qke->qrk", queries, gathered[..., :E], preferred_element_type=jnp.float32
        ) * E ** (-0.5)
        scores = jnp.where(live_cols, raw_scores, -jnp.inf)
        row_peak = jnp.max(scores, axis=-1, keepdims=True)
        log_total = row_peak + jnp.log(jnp.sum(jnp.exp(scores - row_peak), axis=-1, keepdims=True))
        weights = jnp.exp(scores - log_total).astype(jnp.bfloat16)
        attention_output = jnp.einsum(
            "qrk,qke->qre", weights, gathered[..., E:], preferred_element_type=jnp.float32
        ).astype(jnp.bfloat16)
        saved.append(
            (item_head, segment, queries, gathered, item_blocks, weights, attention_output)
        )
    segment_ids = [entry[1] for entry in saved]
    attended_send = place_items([entry[6] for entry in saved], segment_ids, slot_total, segments)
    attended_back = lax.all_to_all(attended_send, "seq", split_axis=1, concat_axis=1, tiled=True)
    attention_output_rows = collect_heads(attended_back, sources, shard_rows)
    adapter_projected = jnp.dot(
        attention_output_rows, adapter_down_weight, preferred_element_type=jnp.float32
    ).astype(jnp.bfloat16)
    fetched_rows = jnp.einsum(
        "ec,sc->es", output_gradient, adapter_up_weight, preferred_element_type=jnp.float32
    ).astype(jnp.bfloat16)
    attention_output_gradient = (
        output_gradient.astype(jnp.float32)
        + jnp.einsum(
            "ab,eb->ae", fetched_rows, adapter_down_weight, preferred_element_type=jnp.float32
        )
    ).astype(jnp.bfloat16)
    cotangent_in = lax.all_to_all(
        spread_rows(attention_output_gradient, targets),
        "seq",
        split_axis=0,
        concat_axis=0,
        tiled=True,
    )
    down_term = jnp.einsum(
        "td,tr->dr", attention_output_rows, fetched_rows, preferred_element_type=jnp.float32
    )
    up_term = jnp.einsum(
        "tr,td->rd", adapter_projected, output_gradient, preferred_element_type=jnp.float32
    )
    grad_down, grad_up = lax.psum((down_term, up_term), "seq")
    rescale = (shard_rows * device_total) ** (-0.5)
    cotangent_by_source = cotangent_in.reshape(per_source, segments, slot_total, shard_rows, E)
    key_sums = jnp.zeros((head_slots, block_total, BLOCK, E), jnp.float32)
    value_sums = jnp.zeros((head_slots, block_total, BLOCK, E), jnp.float32)
    query_pieces = []
    for within in range(ITEMS_DEV):
        item_head, segment, queries, gathered, item_blocks, weights, attention_output = saved[
            within
        ]
        grad_item = lax.dynamic_index_in_dim(cotangent_by_source, segment, 1, False)[
            :, within // segments
        ]
        value_grad = jnp.einsum(
            "qrk,qre->qke", weights, grad_item, preferred_element_type=jnp.float32
        )
        dotted = jnp.einsum(
            "qre,qke->qrk", grad_item, gathered[..., E:], preferred_element_type=jnp.float32
        ).astype(jnp.bfloat16)
        row_delta = jnp.sum(
            grad_item.astype(jnp.float32) * attention_output.astype(jnp.float32),
            axis=-1,
            keepdims=True,
        )
        score_grad = (
            weights.astype(jnp.float32) * (dotted.astype(jnp.float32) - row_delta)
        ).astype(jnp.bfloat16)
        query_grad = (
            jnp.einsum(
                "qrk,qke->qre", score_grad, gathered[..., :E], preferred_element_type=jnp.float32
            )
            * E ** (-0.5)
        ).astype(jnp.bfloat16)
        key_grad = jnp.einsum(
            "qrk,qre->qke", score_grad, queries, preferred_element_type=jnp.float32
        ) * E ** (-0.5)
        slot_now = item_head - first_head
        key_sums = key_sums.at[slot_now, item_blocks].add(key_grad.reshape(-1, KB, BLOCK, E))
        value_sums = value_sums.at[slot_now, item_blocks].add(value_grad.reshape(-1, KB, BLOCK, E))
        query_pieces.append(query_grad)
    query_send_back = place_items(query_pieces, segment_ids, slot_total, segments)
    keyval_send_back = (
        jnp.concatenate([key_sums, value_sums], axis=-1)
        .astype(jnp.bfloat16)
        .reshape(head_slots, device_total, shard_rows * 2 * E)
    )
    query_back, keyval_back = (
        lax.all_to_all(query_send_back, "seq", split_axis=1, concat_axis=1, tiled=True),
        lax.all_to_all(keyval_send_back, "seq", split_axis=1, concat_axis=1, tiled=True),
    )
    query_rows = collect_heads(query_back, sources, shard_rows)
    stacked = jnp.concatenate(
        [
            keyval_back.reshape(head_slots * device_total, shard_rows * 2 * E),
            jnp.zeros((1, shard_rows * 2 * E), jnp.bfloat16),
        ],
        axis=0,
    )
    summed = jnp.sum(
        jnp.take(stacked, jnp.asarray(contributors), axis=0), axis=1, dtype=jnp.float32
    ).astype(jnp.bfloat16)
    keyval_rows = jnp.transpose(summed.reshape(H, shard_rows, 2 * E), (1, 0, 2))
    key_rows = keyval_rows[..., :E].reshape(shard_rows, H * E)
    value_rows = keyval_rows[..., E:].reshape(shard_rows, H * E)
    grad_qkv = jnp.concatenate([query_rows, key_rows, value_rows], axis=1)
    return (grad_qkv, grad_down * rescale, grad_up * rescale)


LOG2E = 1.4426950408889634
ROLL = E


def low_lanes(rows):
    return lax.broadcasted_iota(jnp.int32, (rows, 2 * E), 1) < E


def swap(tile):
    return pltpu.roll(tile, ROLL, 1)


def pack_kernel(qkv_ref, grad_ref, up_ref, send_ref, pulled_ref):
    low = low_lanes(BLOCK)
    for pair in range(H // 2):
        at = pair * 2 * E
        query, key, value = (
            qkv_ref[:, part * H * E + at : part * H * E + at + 2 * E].astype(jnp.float32)
            for part in range(3)
        )
        grad = grad_ref[:, at : at + 2 * E].astype(jnp.float32)
        for left, right, half in ((grad, query, 0), (value, key, 1)):
            lanes = slice(half * 2 * E, half * 2 * E + 2 * E)
            send_ref[2 * pair, :, lanes] = jnp.where(low, left, swap(right)).astype(jnp.bfloat16)
            send_ref[2 * pair + 1, :, lanes] = jnp.where(low, swap(left), right).astype(
                jnp.bfloat16
            )
    pulled_ref[...] = lax.dot_general(
        grad_ref[...], up_ref[...], (((1,), (1,)), ((), ())), preferred_element_type=jnp.float32
    ).astype(jnp.bfloat16)


def head_kernel(
    lists_ref, counts_ref, packed_ref, pulled_ref, wide_ref, down_ref,
    out_ref, grad_down_ref,
    sums, adapted, flipped, flipped_keyval, gathered, gathered_flip, attended, lowrank,
):
    head = pl.program_id(0)
    block_total = packed_ref.shape[0]
    low = low_lanes(BLOCK)
    top = lax.broadcasted_iota(jnp.int32, (2 * E, BLOCK), 0) < E
    live = counts_ref[head]

    def prepare(block, carry):
        rows = pl.ds(pl.multiple_of(block * BLOCK, BLOCK), BLOCK)
        grad_query = packed_ref[block, 0, :, : 2 * E].astype(jnp.float32)
        extra = jnp.dot(pulled_ref[rows, :], wide_ref[0], preferred_element_type=jnp.float32)
        full = (grad_query + extra).astype(jnp.bfloat16)
        adapted[block] = full
        flipped[block] = full.astype(jnp.float32).T.astype(jnp.bfloat16)
        flipped_keyval[block] = (
            packed_ref[block, 0, :, 2 * E :].astype(jnp.float32).T.astype(jnp.bfloat16)
        )
        sums[head, block] = jnp.zeros((BLOCK, 2 * E), jnp.float32)
        return carry

    lax.fori_loop(0, block_total, prepare, 0)

    def attend(block, carry):
        cols = pl.ds(pl.multiple_of(block * BLOCK, BLOCK), BLOCK)
        zero = jnp.zeros((BLOCK, 2 * E), jnp.bfloat16)
        for slot in range(KB):
            listed = lists_ref[head, block, slot]
            gathered[slot * BLOCK : (slot + 1) * BLOCK, :] = packed_ref[listed, 0, :, 2 * E :]
            gathered_flip[:, slot * BLOCK : (slot + 1) * BLOCK] = flipped_keyval[listed]
        turned = flipped[block]
        pair = jnp.concatenate([jnp.where(top, turned, zero), jnp.where(top, zero, turned)], axis=1)
        both = jnp.dot(gathered[...], pair, preferred_element_type=jnp.float32)
        dotted = both[:, :BLOCK]
        slots = lax.broadcasted_iota(jnp.int32, (KB * BLOCK, BLOCK), 0)
        scores = jnp.where(slots < live * BLOCK, both[:, BLOCK:], -jnp.inf)
        peak = jnp.max(scores, axis=0, keepdims=True)
        raised = jnp.exp2((scores - peak) * (LOG2E * E**-0.5))
        weights = (raised * (1.0 / jnp.sum(raised, axis=0, keepdims=True))).astype(jnp.bfloat16)
        output = jnp.dot(
            gathered_flip[:E, :], weights, preferred_element_type=jnp.float32
        ).astype(jnp.bfloat16)
        attended[:, cols] = output
        delta = jnp.sum(
            output.astype(jnp.float32) * turned[:E].astype(jnp.float32), axis=0, keepdims=True
        )
        score_grad = (weights.astype(jnp.float32) * (dotted - delta)).astype(jnp.bfloat16)
        query_grad = (
            jnp.dot(gathered_flip[E:, :], score_grad, preferred_element_type=jnp.float32)
            * E**-0.5
        )
        query_wide = jnp.concatenate([query_grad, jnp.zeros_like(query_grad)], axis=0).T
        out_ref[block, head] = query_wide.astype(jnp.bfloat16)
        mixed = adapted[block]
        stacked = jnp.concatenate([jnp.where(low, mixed, zero), jnp.where(low, zero, mixed)], axis=0)
        partial = jnp.dot(
            jnp.concatenate([weights, score_grad], axis=1),
            stacked,
            preferred_element_type=jnp.float32,
        )
        for slot in range(KB):
            listed = lists_ref[head, block, slot]
            sums[head, listed] += partial[slot * BLOCK : (slot + 1) * BLOCK]
        return carry

    lax.fori_loop(0, block_total, attend, 0)

    def finish(block, carry):
        key_value = sums[head, block]
        out_ref[block, head] = jnp.where(
            low, out_ref[block, head].astype(jnp.float32), key_value * E**-0.5
        ).astype(jnp.bfloat16)
        return carry

    lax.fori_loop(0, block_total, finish, 0)
    grad_down_ref[0] = jnp.dot(
        attended[...], pulled_ref[...], preferred_element_type=jnp.float32
    ) * (block_total * BLOCK) ** (-0.5)
    term = lax.dot_general(
        down_ref[0], attended[...], (((0,), (0,)), ((), ())), preferred_element_type=jnp.float32
    )

    @pl.when(head == 0)
    def _():
        lowrank[...] = term

    @pl.when(head > 0)
    def _():
        lowrank[...] += term

    @pl.when(head == ITEMS_DEV - 1)
    def _():
        def tail(block, carry):
            cols = pl.ds(pl.multiple_of(block * BLOCK, BLOCK), BLOCK)
            out_ref[block, 3] = jnp.where(low, sums[0, block], swap(sums[1, block])).astype(
                jnp.bfloat16
            )
            rank = lowrank[:, cols]
            rank = jnp.concatenate([jnp.zeros_like(rank), rank], axis=0).T
            out_ref[block, 4] = jnp.where(low, sums[2, block], rank).astype(jnp.bfloat16)
            return carry

        lax.fori_loop(0, block_total, tail, 0)


def unpack_kernel(back_ref, out_ref, lowrank_ref):
    low = low_lanes(BLOCK)
    total = jnp.zeros((BLOCK, 2 * E), jnp.float32)

    def tile(device, which):
        return back_ref[device, which].astype(jnp.float32)

    for pair in range(H // 2):
        at = pair * 2 * E
        first, second = 2 * pair, 2 * pair + 1
        left = tile(first // ITEMS_DEV, first % ITEMS_DEV)
        right = tile(second // ITEMS_DEV, second % ITEMS_DEV)
        out_ref[:, at : at + 2 * E] = jnp.where(low, left, swap(right)).astype(jnp.bfloat16)
        out_ref[:, H * E + at : H * E + at + 2 * E] = jnp.where(low, swap(left), right).astype(
            jnp.bfloat16
        )
        placed = []
        for head, want in ((first, 0), (second, 1)):
            device, within = head // ITEMS_DEV, head % ITEMS_DEV
            value = tile(device, 3 + within // 2)
            placed.append(value if within % 2 == want else swap(value))
        out_ref[:, 2 * H * E + at : 2 * H * E + at + 2 * E] = jnp.where(
            low, placed[0], placed[1]
        ).astype(jnp.bfloat16)
    for device in range(back_ref.shape[0]):
        total += tile(device, 4)
    lowrank_ref[...] = total[:, E:].astype(jnp.bfloat16)


def whole_heads(
    qkv, output_gradient, adapter_down_weight, adapter_up_weight, listed_key_blocks, key_block_count
):
    device_total = lax.axis_size("seq")
    me = lax.axis_index("seq")
    vmem = pl.BlockSpec(memory_space=pltpu.VMEM)
    params = pltpu.CompilerParams(vmem_limit_bytes=48 * 1024 * 1024)
    send, pulled = pl.pallas_call(
        pack_kernel,
        out_shape=(
            jax.ShapeDtypeStruct((H, BLOCK, 4 * E), jnp.bfloat16),
            jax.ShapeDtypeStruct((BLOCK, adapter_up_weight.shape[0]), jnp.bfloat16),
        ),
        in_specs=[vmem] * 3,
        out_specs=(vmem, vmem),
        compiler_params=params,
    )(qkv, output_gradient, adapter_up_weight)
    pulled_all = lax.all_gather(pulled, "seq", axis=0, tiled=True)
    packed = lax.all_to_all(
        send.reshape(device_total, ITEMS_DEV, BLOCK, 4 * E), "seq", 0, 0, tiled=True
    )
    first = me * ITEMS_DEV
    lists = lax.dynamic_slice_in_dim(listed_key_blocks, first, ITEMS_DEV, 0)
    counts = lax.dynamic_slice_in_dim(key_block_count, first, ITEMS_DEV, 0)
    down = lax.dynamic_slice_in_dim(adapter_down_weight, first * E, ITEMS_DEV * E, 0).reshape(
        ITEMS_DEV, E, -1
    )
    rank = down.shape[-1]
    wide = jnp.pad(jnp.swapaxes(down, 1, 2), ((0, 0), (0, 0), (0, E)))
    tokens = device_total * BLOCK
    back, grad_down = pl.pallas_call(
        head_kernel,
        grid_spec=pltpu.PrefetchScalarGridSpec(
            num_scalar_prefetch=2,
            grid=(ITEMS_DEV,),
            in_specs=[
                pl.BlockSpec((device_total, 1, BLOCK, 4 * E), lambda h, *_: (0, h, 0, 0)),
                pl.BlockSpec((tokens, rank), lambda h, *_: (0, 0)),
                pl.BlockSpec((1, rank, 2 * E), lambda h, *_: (h, 0, 0)),
                pl.BlockSpec((1, E, rank), lambda h, *_: (h, 0, 0)),
            ],
            out_specs=[
                pl.BlockSpec((device_total, 5, BLOCK, 2 * E), lambda h, *_: (0, 0, 0, 0)),
                pl.BlockSpec((1, E, rank), lambda h, *_: (h, 0, 0)),
            ],
            scratch_shapes=[
                pltpu.VMEM((ITEMS_DEV, device_total, BLOCK, 2 * E), jnp.float32),
                pltpu.VMEM((device_total, BLOCK, 2 * E), jnp.bfloat16),
                pltpu.VMEM((device_total, 2 * E, BLOCK), jnp.bfloat16),
                pltpu.VMEM((device_total, 2 * E, BLOCK), jnp.bfloat16),
                pltpu.VMEM((KB * BLOCK, 2 * E), jnp.bfloat16),
                pltpu.VMEM((2 * E, KB * BLOCK), jnp.bfloat16),
                pltpu.VMEM((E, tokens), jnp.bfloat16),
                pltpu.VMEM((rank, tokens), jnp.float32),
            ],
        ),
        out_shape=[
            jax.ShapeDtypeStruct((device_total, 5, BLOCK, 2 * E), jnp.bfloat16),
            jax.ShapeDtypeStruct((ITEMS_DEV, E, rank), jnp.float32),
        ],
        compiler_params=params,
    )(lists, counts, packed, pulled_all, wide, down)
    grad_down_all = lax.all_gather(
        grad_down.reshape(ITEMS_DEV * E, rank), "seq", axis=0, tiled=True
    )
    returned = lax.all_to_all(back, "seq", 0, 0, tiled=True)
    grad_qkv, lowrank = pl.pallas_call(
        unpack_kernel,
        out_shape=(
            jax.ShapeDtypeStruct(qkv.shape, jnp.bfloat16),
            jax.ShapeDtypeStruct((BLOCK, rank), jnp.bfloat16),
        ),
        in_specs=[vmem],
        out_specs=(vmem, vmem),
        compiler_params=params,
    )(returned)
    lowrank_all = lax.all_gather(lowrank, "seq", axis=0, tiled=True)
    grad_up = jnp.einsum(
        "str,shte->her",
        lowrank_all.reshape(device_total, BLOCK, rank),
        packed[..., :E].astype(jnp.bfloat16),
        preferred_element_type=jnp.float32,
    ) * tokens ** (-0.5)
    grad_up_all = lax.all_gather(
        grad_up.reshape(ITEMS_DEV * E, rank), "seq", axis=0, tiled=True
    )
    return (grad_qkv, grad_down_all, grad_up_all.T)


def shards(qkv, *others):
    if ITEMS_DEV * lax.axis_size("seq") == H and qkv.shape[0] == BLOCK:
        return whole_heads(qkv, *others)
    return segmented(qkv, *others)


def solution(mesh):
    return jax.shard_map(
        shards,
        mesh=mesh,
        in_specs=(P(("groups", "seq"), None), P(("groups", "seq"), None), P(), P(), P(), P()),
        out_specs=(P(("groups", "seq"), None), P("groups", None), P("groups", None)),
        check_vma=False,
    )
```

```python
import functools

import jax
import jax.numpy as jnp
import numpy as np
from jax import lax
from jax.experimental import pallas as pl
from jax.experimental.pallas import tpu as pltpu
from jax.sharding import PartitionSpec as P

H = 48
E = 64
BLOCK = 128
KB = 10
ITEMS_DEV = 3


def tables(device_total, segments):
    slot_total = -(-ITEMS_DEV // segments)
    head_slots = min(ITEMS_DEV, (ITEMS_DEV + segments - 2) // segments + 1)
    device = np.repeat(np.arange(device_total), ITEMS_DEV)
    within = np.tile(np.arange(ITEMS_DEV), device_total)
    item_id = device * ITEMS_DEV + within
    head_for = np.full((segments, device_total, slot_total), H, np.int32)
    head_for[item_id % segments, device, within // segments] = item_id // segments
    source_for = np.zeros((segments, H), np.int32)
    source_for[item_id % segments, item_id // segments] = within // segments * device_total + device
    item_heads = (item_id // segments).reshape(device_total, ITEMS_DEV).astype(np.int32)
    first_head = np.arange(device_total) * ITEMS_DEV // segments
    last_head = (np.arange(device_total) * ITEMS_DEV + ITEMS_DEV - 1) // segments
    slot_heads = np.minimum(
        first_head[:, None] + np.arange(head_slots)[None, :], last_head[:, None]
    ).astype(np.int32)
    owned_heads = []
    owned_rows = []
    for slot_pos in range(head_slots):
        usable = first_head + slot_pos <= last_head
        owned_heads.append((first_head + slot_pos)[usable])
        owned_rows.append((slot_pos * device_total + np.arange(device_total))[usable])
    owned_heads = np.concatenate(owned_heads)
    owned_rows = np.concatenate(owned_rows)
    ordering = np.argsort(owned_heads, kind="stable")
    sorted_heads = owned_heads[ordering]
    sorted_rows = owned_rows[ordering]
    position = np.arange(sorted_heads.size) - np.searchsorted(sorted_heads, sorted_heads)
    contributors = np.full((H, int(position.max()) + 1), head_slots * device_total, np.int32)
    contributors[sorted_heads, position] = sorted_rows
    return (head_for, source_for, item_heads, slot_heads, contributors)


def spread_rows(features, targets):
    shard_rows = features.shape[0]
    per_head = jnp.transpose(features.reshape(shard_rows, H, E), (1, 0, 2))
    padded = jnp.concatenate([per_head, jnp.zeros((1, shard_rows, E), features.dtype)], axis=0)
    return jnp.take(padded, targets, axis=0).reshape(targets.shape[0], -1)


def collect_heads(received, sources, shard_rows):
    flattened = received.reshape(-1, shard_rows * E)
    picked = jnp.take(flattened, sources, axis=0)
    return jnp.transpose(picked.reshape(H, shard_rows, E), (1, 0, 2)).reshape(shard_rows, H * E)


def place_items(pieces, segment_ids, slot_total, segments):
    per_source = pieces[0].shape[0]
    buffer = jnp.zeros((slot_total, per_source, segments, pieces[0][0].size), jnp.bfloat16)
    anchor = jnp.zeros((), jnp.int32)
    for within in range(len(pieces)):
        update = pieces[within].reshape(1, per_source, 1, -1)
        slot_start = jnp.full((), within // segments, jnp.int32)
        buffer = lax.dynamic_update_slice(
            buffer, update, (slot_start, anchor, segment_ids[within], anchor)
        )
    return buffer.reshape(slot_total, per_source * segments, -1)


def segmented(
    qkv, output_gradient, adapter_down_weight, adapter_up_weight, listed_key_blocks, key_block_count
):
    device_total = lax.axis_size("seq")
    my_index = lax.axis_index("seq")
    shard_rows = qkv.shape[0]
    segments = ITEMS_DEV * device_total // H
    slot_total = -(-ITEMS_DEV // segments)
    per_source = device_total // segments
    blocks_per_shard = shard_rows // BLOCK
    block_total = device_total * blocks_per_shard
    head_for, source_for, item_heads, slot_heads, contributors = tables(device_total, segments)
    head_slots = slot_heads.shape[1]
    residue = my_index % segments
    targets = lax.dynamic_index_in_dim(jnp.asarray(head_for), residue, 0, False)
    sources = lax.dynamic_index_in_dim(jnp.asarray(source_for), residue, 0, False)
    query_send = spread_rows(qkv[:, : H * E], targets)
    key_part = qkv[:, H * E : 2 * H * E].reshape(shard_rows, H, E)
    value_part = qkv[:, 2 * H * E :].reshape(shard_rows, H, E)
    keyval_heads = jnp.transpose(
        jnp.concatenate([key_part, value_part], axis=2), (1, 0, 2)
    ).reshape(H, shard_rows * 2 * E)
    first_head = my_index * ITEMS_DEV // segments
    received_queries, received_keyval = (
        lax.all_to_all(query_send, "seq", split_axis=0, concat_axis=0, tiled=True),
        lax.all_to_all(
            jnp.take(keyval_heads, jnp.asarray(item_heads), axis=0),
            "seq",
            split_axis=0,
            concat_axis=0,
            tiled=True,
        ),
    )
    queries_by_source = received_queries.reshape(per_source, segments, slot_total, shard_rows, E)
    keyval_by_slot = received_keyval.reshape(device_total, -1, shard_rows * 2 * E)
    source_ids = jnp.arange(per_source, dtype=jnp.int32)
    column_block = jnp.arange(KB * BLOCK, dtype=jnp.int32) // BLOCK
    saved = []
    for within in range(ITEMS_DEV):
        item_id = my_index * ITEMS_DEV + within
        item_head = item_id // segments
        segment = item_id % segments
        queries = lax.dynamic_index_in_dim(queries_by_source, segment, 1, False)[
            :, within // segments
        ]
        query_ids = (
            (segment + segments * source_ids)[:, None] * blocks_per_shard
            + jnp.arange(blocks_per_shard, dtype=jnp.int32)[None, :]
        ).reshape(-1)
        item_blocks = jnp.take(
            lax.dynamic_index_in_dim(listed_key_blocks, item_head, 0, False), query_ids, axis=0
        )
        keyval_item = lax.dynamic_index_in_dim(keyval_by_slot, within, 1, False).reshape(
            block_total, BLOCK, 2 * E
        )
        gathered = jnp.take(keyval_item, item_blocks, axis=0).reshape(-1, KB * BLOCK, 2 * E)
        live_cols = column_block < key_block_count[item_head]
        raw_scores = jnp.einsum(
            "qre,qke->qrk", queries, gathered[..., :E], preferred_element_type=jnp.float32
        ) * E ** (-0.5)
        scores = jnp.where(live_cols, raw_scores, -jnp.inf)
        row_peak = jnp.max(scores, axis=-1, keepdims=True)
        log_total = row_peak + jnp.log(jnp.sum(jnp.exp(scores - row_peak), axis=-1, keepdims=True))
        weights = jnp.exp(scores - log_total).astype(jnp.bfloat16)
        attention_output = jnp.einsum(
            "qrk,qke->qre", weights, gathered[..., E:], preferred_element_type=jnp.float32
        ).astype(jnp.bfloat16)
        saved.append(
            (item_head, segment, queries, gathered, item_blocks, weights, attention_output)
        )
    segment_ids = [entry[1] for entry in saved]
    attended_send = place_items([entry[6] for entry in saved], segment_ids, slot_total, segments)
    attended_back = lax.all_to_all(attended_send, "seq", split_axis=1, concat_axis=1, tiled=True)
    attention_output_rows = collect_heads(attended_back, sources, shard_rows)
    adapter_projected = jnp.dot(
        attention_output_rows, adapter_down_weight, preferred_element_type=jnp.float32
    ).astype(jnp.bfloat16)
    fetched_rows = jnp.einsum(
        "ec,sc->es", output_gradient, adapter_up_weight, preferred_element_type=jnp.float32
    ).astype(jnp.bfloat16)
    attention_output_gradient = (
        output_gradient.astype(jnp.float32)
        + jnp.einsum(
            "ab,eb->ae", fetched_rows, adapter_down_weight, preferred_element_type=jnp.float32
        )
    ).astype(jnp.bfloat16)
    cotangent_in = lax.all_to_all(
        spread_rows(attention_output_gradient, targets),
        "seq",
        split_axis=0,
        concat_axis=0,
        tiled=True,
    )
    down_term = jnp.einsum(
        "td,tr->dr", attention_output_rows, fetched_rows, preferred_element_type=jnp.float32
    )
    up_term = jnp.einsum(
        "tr,td->rd", adapter_projected, output_gradient, preferred_element_type=jnp.float32
    )
    grad_down, grad_up = lax.psum((down_term, up_term), "seq")
    rescale = (shard_rows * device_total) ** (-0.5)
    cotangent_by_source = cotangent_in.reshape(per_source, segments, slot_total, shard_rows, E)
    key_sums = jnp.zeros((head_slots, block_total, BLOCK, E), jnp.float32)
    value_sums = jnp.zeros((head_slots, block_total, BLOCK, E), jnp.float32)
    query_pieces = []
    for within in range(ITEMS_DEV):
        item_head, segment, queries, gathered, item_blocks, weights, attention_output = saved[
            within
        ]
        grad_item = lax.dynamic_index_in_dim(cotangent_by_source, segment, 1, False)[
            :, within // segments
        ]
        value_grad = jnp.einsum(
            "qrk,qre->qke", weights, grad_item, preferred_element_type=jnp.float32
        )
        dotted = jnp.einsum(
            "qre,qke->qrk", grad_item, gathered[..., E:], preferred_element_type=jnp.float32
        ).astype(jnp.bfloat16)
        row_delta = jnp.sum(
            grad_item.astype(jnp.float32) * attention_output.astype(jnp.float32),
            axis=-1,
            keepdims=True,
        )
        score_grad = (
            weights.astype(jnp.float32) * (dotted.astype(jnp.float32) - row_delta)
        ).astype(jnp.bfloat16)
        query_grad = (
            jnp.einsum(
                "qrk,qke->qre", score_grad, gathered[..., :E], preferred_element_type=jnp.float32
            )
            * E ** (-0.5)
        ).astype(jnp.bfloat16)
        key_grad = jnp.einsum(
            "qrk,qre->qke", score_grad, queries, preferred_element_type=jnp.float32
        ) * E ** (-0.5)
        slot_now = item_head - first_head
        key_sums = key_sums.at[slot_now, item_blocks].add(key_grad.reshape(-1, KB, BLOCK, E))
        value_sums = value_sums.at[slot_now, item_blocks].add(value_grad.reshape(-1, KB, BLOCK, E))
        query_pieces.append(query_grad)
    query_send_back = place_items(query_pieces, segment_ids, slot_total, segments)
    keyval_send_back = (
        jnp.concatenate([key_sums, value_sums], axis=-1)
        .astype(jnp.bfloat16)
        .reshape(head_slots, device_total, shard_rows * 2 * E)
    )
    query_back, keyval_back = (
        lax.all_to_all(query_send_back, "seq", split_axis=1, concat_axis=1, tiled=True),
        lax.all_to_all(keyval_send_back, "seq", split_axis=1, concat_axis=1, tiled=True),
    )
    query_rows = collect_heads(query_back, sources, shard_rows)
    stacked = jnp.concatenate(
        [
            keyval_back.reshape(head_slots * device_total, shard_rows * 2 * E),
            jnp.zeros((1, shard_rows * 2 * E), jnp.bfloat16),
        ],
        axis=0,
    )
    summed = jnp.sum(
        jnp.take(stacked, jnp.asarray(contributors), axis=0), axis=1, dtype=jnp.float32
    ).astype(jnp.bfloat16)
    keyval_rows = jnp.transpose(summed.reshape(H, shard_rows, 2 * E), (1, 0, 2))
    key_rows = keyval_rows[..., :E].reshape(shard_rows, H * E)
    value_rows = keyval_rows[..., E:].reshape(shard_rows, H * E)
    grad_qkv = jnp.concatenate([query_rows, key_rows, value_rows], axis=1)
    return (grad_qkv, grad_down * rescale, grad_up * rescale)


LOG2E = 1.4426950408889634
ROLL = E


def low_lanes(rows):
    return lax.broadcasted_iota(jnp.int32, (rows, 2 * E), 1) < E


def swap(tile):
    return pltpu.roll(tile, ROLL, 1)


def pack_kernel(qkv_ref, grad_ref, up_ref, *send_refs):
    low = low_lanes(BLOCK)
    for pair in range(H // 2):
        at = pair * 2 * E
        query, key, value = (
            qkv_ref[:, part * H * E + at : part * H * E + at + 2 * E].astype(jnp.float32)
            for part in range(3)
        )
        grad = grad_ref[:, at : at + 2 * E].astype(jnp.float32)
        for left, right, half in ((grad, query, 0), (value, key, 1)):
            lanes = slice(half * 2 * E, half * 2 * E + 2 * E)
            for head, tile in (
                (2 * pair, jnp.where(low, left, swap(right))),
                (2 * pair + 1, jnp.where(low, swap(left), right)),
            ):
                send_refs[head % ITEMS_DEV][head // ITEMS_DEV, :BLOCK, lanes] = tile.astype(
                    jnp.bfloat16
                )
    pulled = lax.dot_general(
        grad_ref[...], up_ref[...], (((1,), (1,)), ((), ())), preferred_element_type=jnp.float32
    )
    folded = jnp.concatenate(
        [pulled[part * BLOCK // 4 : (part + 1) * BLOCK // 4] for part in range(4)], axis=1
    ).astype(jnp.bfloat16)
    for device in range(send_refs[0].shape[0]):
        send_refs[0][device, BLOCK:, :] = folded


def head_kernel(forward, backward, unfold, *refs):
    refs = list(refs)
    lists_ref, counts_ref, packed_ref, wide_ref, down_ref = refs[:5]
    del refs[:5]
    block_total = packed_ref.shape[0]
    pulled_in = None if unfold else refs.pop(0)
    lowrank_in = refs.pop(0) if forward and not unfold else None
    if backward:
        rows_ref, sums = refs.pop(0), refs.pop(0)
    if unfold:
        pulled_ref = refs.pop(0)
    else:
        pulled_ref = pulled_in
    if forward:
        grad_down_ref, lowrank_ref = refs.pop(0), refs.pop(0)
    adapted, flipped, flipped_keyval, gathered, gathered_flip, attended = refs
    low = low_lanes(BLOCK)
    top = lax.broadcasted_iota(jnp.int32, (2 * E, BLOCK), 0) < E
    live = counts_ref[0]
    zero = jnp.zeros((BLOCK, 2 * E), jnp.bfloat16)

    def prepare(block, carry):
        rows = pl.ds(pl.multiple_of(block * BLOCK, BLOCK), BLOCK)
        if unfold:
            folded = packed_ref[block, BLOCK:, :]
            pulled_ref[rows, :] = jnp.concatenate(
                [folded[:, part * E : (part + 1) * E] for part in range(4)], axis=0
            )
        grad_query = packed_ref[block, :BLOCK, : 2 * E].astype(jnp.float32)
        extra = jnp.dot(pulled_ref[rows, :], wide_ref[...], preferred_element_type=jnp.float32)
        full = (grad_query + extra).astype(jnp.bfloat16)
        adapted[block] = full
        flipped[block] = full.astype(jnp.float32).T.astype(jnp.bfloat16)
        flipped_keyval[block] = (
            packed_ref[block, :BLOCK, 2 * E :].astype(jnp.float32).T.astype(jnp.bfloat16)
        )
        if backward:
            sums[block] = jnp.zeros((BLOCK, 2 * E), jnp.float32)
        return carry

    lax.fori_loop(0, block_total, prepare, 0)

    def attend(step, carry):
        blocks = [2 * step, 2 * step + 1]
        for side, block in enumerate(blocks):
            for slot in range(KB):
                listed = lists_ref[block, slot]
                span = slice(slot * BLOCK, (slot + 1) * BLOCK)
                gathered[side, span, :] = packed_ref[listed, :BLOCK, 2 * E :]
                gathered_flip[side, :, span] = flipped_keyval[listed]
        turned = [flipped[block] for block in blocks]
        both = []
        for side in range(2):
            pair = jnp.concatenate(
                [jnp.where(top, turned[side], zero), jnp.where(top, zero, turned[side])], axis=1
            )
            both.append(jnp.dot(gathered[side], pair, preferred_element_type=jnp.float32))
        slots = lax.broadcasted_iota(jnp.int32, (KB * BLOCK, BLOCK), 0)
        weights = []
        for side in range(2):
            scores = jnp.where(slots < live * BLOCK, both[side][:, BLOCK:], -jnp.inf)
            peak = jnp.max(scores, axis=0, keepdims=True)
            raised = jnp.exp2((scores - peak) * (LOG2E * E**-0.5))
            weights.append(
                (raised * (1.0 / jnp.sum(raised, axis=0, keepdims=True))).astype(jnp.bfloat16)
            )
        outputs = [
            jnp.dot(
                gathered_flip[side, :E, :], weights[side], preferred_element_type=jnp.float32
            ).astype(jnp.bfloat16)
            for side in range(2)
        ]
        if forward:
            cols = pl.ds(pl.multiple_of(step * 2 * BLOCK, 2 * BLOCK), 2 * BLOCK)
            attended[:, cols] = jnp.concatenate(outputs, axis=1)
        if not backward:
            return carry
        score_grads = []
        for side in range(2):
            delta = jnp.sum(
                outputs[side].astype(jnp.float32) * turned[side][:E].astype(jnp.float32),
                axis=0,
                keepdims=True,
            )
            score_grads.append(
                (weights[side].astype(jnp.float32) * (both[side][:, :BLOCK] - delta)).astype(
                    jnp.bfloat16
                )
            )
        partials = []
        for side, block in enumerate(blocks):
            query_grad = (
                jnp.dot(
                    gathered_flip[side, E:, :],
                    score_grads[side],
                    preferred_element_type=jnp.float32,
                )
                * E**-0.5
            )
            rows_ref[block] = jnp.concatenate(
                [query_grad, jnp.zeros_like(query_grad)], axis=0
            ).T.astype(jnp.bfloat16)
            mixed = adapted[block]
            stacked = jnp.concatenate(
                [jnp.where(low, mixed, zero), jnp.where(low, zero, mixed)], axis=0
            )
            partials.append(
                jnp.dot(
                    jnp.concatenate([weights[side], score_grads[side]], axis=1),
                    stacked,
                    preferred_element_type=jnp.float32,
                )
            )
        for side, block in enumerate(blocks):
            for slot in range(KB):
                listed = lists_ref[block, slot]
                sums[listed] += partials[side][slot * BLOCK : (slot + 1) * BLOCK]
        return carry

    lax.fori_loop(0, block_total // 2, attend, 0)

    if backward:
        def finish(block, carry):
            rows_ref[block] = jnp.where(
                low, rows_ref[block].astype(jnp.float32), sums[block] * E**-0.5
            ).astype(jnp.bfloat16)
            return carry

        lax.fori_loop(0, block_total, finish, 0)
    if forward:
        grad_down_ref[...] = jnp.dot(
            attended[...], pulled_ref[...], preferred_element_type=jnp.float32
        ) * (block_total * BLOCK) ** (-0.5)
        term = lax.dot_general(
            down_ref[...], attended[...], (((0,), (0,)), ((), ())),
            preferred_element_type=jnp.float32,
        )
        lowrank_ref[...] = term if unfold else term + lowrank_in[...]


def head_pass(forward, backward, unfold, lists, counts, packed, wide, down, *extra):
    blocks = packed.shape[0]
    rank = down.shape[-1]
    tokens = blocks * BLOCK
    vmem = pl.BlockSpec(memory_space=pltpu.VMEM)
    smem = pl.BlockSpec(memory_space=pltpu.SMEM)
    outs = []
    if backward:
        outs.append(jax.ShapeDtypeStruct((blocks, BLOCK, 2 * E), jnp.bfloat16))
        outs.append(jax.ShapeDtypeStruct((blocks, BLOCK, 2 * E), jnp.float32))
    if unfold:
        outs.append(jax.ShapeDtypeStruct((tokens, rank), jnp.bfloat16))
    if forward:
        outs.append(jax.ShapeDtypeStruct((E, rank), jnp.float32))
        outs.append(jax.ShapeDtypeStruct((rank, tokens), jnp.float32))
    return pl.pallas_call(
        functools.partial(head_kernel, forward, backward, unfold),
        out_shape=outs,
        in_specs=[smem, smem] + [vmem] * (3 + len(extra)),
        out_specs=[vmem] * len(outs),
        scratch_shapes=[
            pltpu.VMEM((blocks, BLOCK, 2 * E), jnp.bfloat16),
            pltpu.VMEM((blocks, 2 * E, BLOCK), jnp.bfloat16),
            pltpu.VMEM((blocks, 2 * E, BLOCK), jnp.bfloat16),
            pltpu.VMEM((2, KB * BLOCK, 2 * E), jnp.bfloat16),
            pltpu.VMEM((2, 2 * E, KB * BLOCK), jnp.bfloat16),
            pltpu.VMEM((E, tokens), jnp.bfloat16),
        ],
        compiler_params=pltpu.CompilerParams(vmem_limit_bytes=40 * 1024 * 1024),
        cost_estimate=pl.CostEstimate(
            flops=(20 if backward else 8) * 10**9, bytes_accessed=4 * 10**6, transcendentals=0
        ),
    )(lists, counts, packed, wide, down, *extra)


def rank_kernel(lowrank_ref, first_ref, second_ref, third_ref, out_ref):
    for within, packed_ref in enumerate((first_ref, second_ref, third_ref)):
        total = jnp.zeros((out_ref.shape[1], 2 * E), jnp.float32)
        for block in range(packed_ref.shape[0]):
            total += jnp.dot(
                lowrank_ref[block],
                packed_ref[block, :BLOCK, : 2 * E],
                preferred_element_type=jnp.float32,
            )
        out_ref[within] = total * (packed_ref.shape[0] * BLOCK) ** (-0.5)


def unpack_kernel(early_ref, late_ref, out_ref):
    def tile(device, which):
        if which < 3:
            return early_ref[device, which].astype(jnp.float32)
        return late_ref[device, which - 3].astype(jnp.float32)

    low = low_lanes(BLOCK)
    for pair in range(H // 2):
        at = pair * 2 * E
        left, right = (
            tile(head // ITEMS_DEV, (0, 1, 3)[head % ITEMS_DEV])
            for head in (2 * pair, 2 * pair + 1)
        )
        out_ref[:, at : at + 2 * E] = jnp.where(low, left, swap(right)).astype(jnp.bfloat16)
        out_ref[:, H * E + at : H * E + at + 2 * E] = jnp.where(low, swap(left), right).astype(
            jnp.bfloat16
        )
        placed = []
        for want in range(2):
            head = 2 * pair + want
            device, within = head // ITEMS_DEV, head % ITEMS_DEV
            value = tile(device, 2 if within < 2 else 4)
            placed.append(value if within % 2 == want else swap(value))
        out_ref[:, 2 * H * E + at : 2 * H * E + at + 2 * E] = jnp.where(
            low, placed[0], placed[1]
        ).astype(jnp.bfloat16)


def whole_heads(
    qkv, output_gradient, adapter_down_weight, adapter_up_weight, listed_key_blocks, key_block_count
):
    device_total = lax.axis_size("seq")
    me = lax.axis_index("seq")
    rank = adapter_up_weight.shape[0]
    vmem = pl.BlockSpec(memory_space=pltpu.VMEM)
    params = pltpu.CompilerParams(vmem_limit_bytes=40 * 1024 * 1024)

    def exchange(array):
        return lax.all_to_all(array, "seq", 0, 0, tiled=True)

    sends = pl.pallas_call(
        pack_kernel,
        out_shape=[
            jax.ShapeDtypeStruct(
                (device_total, BLOCK + (BLOCK // 4 if within == 0 else 0), 4 * E), jnp.bfloat16
            )
            for within in range(ITEMS_DEV)
        ],
        in_specs=[vmem] * 3,
        out_specs=[vmem] * ITEMS_DEV,
        compiler_params=params,
    )(qkv, output_gradient, adapter_up_weight)
    packed0 = exchange(sends[0])
    first = me * ITEMS_DEV
    lists = lax.dynamic_slice_in_dim(listed_key_blocks, first, ITEMS_DEV, 0)
    counts = lax.dynamic_slice_in_dim(key_block_count, first, ITEMS_DEV, 0)
    down = lax.dynamic_slice_in_dim(adapter_down_weight, first * E, ITEMS_DEV * E, 0).reshape(
        ITEMS_DEV, E, rank
    )
    wide = jnp.pad(jnp.swapaxes(down, 1, 2), ((0, 0), (0, 0), (0, E)))
    def own(within, packed):
        return (
            lists[within], counts[within : within + 1], packed, wide[within], down[within]
        )

    packed0, send1 = lax.optimization_barrier((packed0, sends[1]))
    packed1 = exchange(send1)
    rows0, sums0, pulled, down0, lowrank = head_pass(True, True, True, *own(0, packed0))
    packed1, rows0, pulled, lowrank, send2 = lax.optimization_barrier(
        (packed1, rows0, pulled, lowrank, sends[2])
    )
    packed2 = exchange(send2)
    rows1, sums1, down1, lowrank = head_pass(
        True, True, False, *own(1, packed1), pulled, lowrank
    )
    values = jnp.concatenate([sums0[..., :E], sums1[..., :E]], axis=-1).astype(jnp.bfloat16)
    early = jnp.stack([rows0, rows1, values], axis=1)
    early, packed2 = lax.optimization_barrier((early, packed2))
    back1 = exchange(early)
    down2, lowrank = head_pass(True, False, False, *own(2, packed2), pulled, lowrank)
    rows2, sums2 = head_pass(False, True, False, *own(2, packed2), pulled)
    spread = jnp.swapaxes(
        lowrank.astype(jnp.bfloat16).reshape(rank, device_total, BLOCK), 0, 1
    )
    late = jnp.stack([rows2, sums2.astype(jnp.bfloat16)], axis=1)
    spread, late, back1 = lax.optimization_barrier((spread, late, back1))
    mine = jnp.sum(exchange(spread), axis=0, dtype=jnp.float32).astype(jnp.bfloat16)
    lowrank_all = exchange(jnp.broadcast_to(mine[None], (device_total, rank, BLOCK)))
    late, lowrank_all = lax.optimization_barrier((late, lowrank_all))
    back2 = exchange(late)
    ups = pl.pallas_call(
        rank_kernel,
        out_shape=jax.ShapeDtypeStruct((ITEMS_DEV, rank, 2 * E), jnp.float32),
        in_specs=[vmem] * 4,
        out_specs=vmem,
        compiler_params=params,
    )(lowrank_all, packed0, packed1, packed2)
    small = jnp.concatenate([jnp.stack([down0, down1, down2]), ups[..., :E]], axis=-1)
    small_all = lax.all_gather(small, "seq", axis=0, tiled=True)
    grad_qkv = pl.pallas_call(
        unpack_kernel,
        out_shape=jax.ShapeDtypeStruct(qkv.shape, jnp.bfloat16),
        in_specs=[vmem] * 2,
        out_specs=vmem,
        compiler_params=params,
    )(back1, back2)
    grad_down = small_all[..., :rank].reshape(H * E, rank)
    grad_up = jnp.swapaxes(small_all[..., rank:], 0, 1).reshape(rank, H * E)
    return (grad_qkv, grad_down, grad_up)


def shards(qkv, *others):
    if ITEMS_DEV * lax.axis_size("seq") == H and qkv.shape[0] == BLOCK:
        return whole_heads(qkv, *others)
    return segmented(qkv, *others)


def solution(mesh):
    return jax.shard_map(
        shards,
        mesh=mesh,
        in_specs=(P(("groups", "seq"), None), P(("groups", "seq"), None), P(), P(), P(), P()),
        out_specs=(P(("groups", "seq"), None), P("groups", None), P("groups", None)),
        check_vma=False,
    )
```

```python
import functools

import jax
import jax.numpy as jnp
import numpy as np
from jax import lax
from jax.experimental import pallas as pl
from jax.experimental.pallas import tpu as pltpu
from jax.sharding import PartitionSpec as P

H = 48
E = 64
BLOCK = 128
KB = 10
ITEMS_DEV = 3


def tables(device_total, segments):
    slot_total = -(-ITEMS_DEV // segments)
    head_slots = min(ITEMS_DEV, (ITEMS_DEV + segments - 2) // segments + 1)
    device = np.repeat(np.arange(device_total), ITEMS_DEV)
    within = np.tile(np.arange(ITEMS_DEV), device_total)
    item_id = device * ITEMS_DEV + within
    head_for = np.full((segments, device_total, slot_total), H, np.int32)
    head_for[item_id % segments, device, within // segments] = item_id // segments
    source_for = np.zeros((segments, H), np.int32)
    source_for[item_id % segments, item_id // segments] = within // segments * device_total + device
    item_heads = (item_id // segments).reshape(device_total, ITEMS_DEV).astype(np.int32)
    first_head = np.arange(device_total) * ITEMS_DEV // segments
    last_head = (np.arange(device_total) * ITEMS_DEV + ITEMS_DEV - 1) // segments
    slot_heads = np.minimum(
        first_head[:, None] + np.arange(head_slots)[None, :], last_head[:, None]
    ).astype(np.int32)
    owned_heads = []
    owned_rows = []
    for slot_pos in range(head_slots):
        usable = first_head + slot_pos <= last_head
        owned_heads.append((first_head + slot_pos)[usable])
        owned_rows.append((slot_pos * device_total + np.arange(device_total))[usable])
    owned_heads = np.concatenate(owned_heads)
    owned_rows = np.concatenate(owned_rows)
    ordering = np.argsort(owned_heads, kind="stable")
    sorted_heads = owned_heads[ordering]
    sorted_rows = owned_rows[ordering]
    position = np.arange(sorted_heads.size) - np.searchsorted(sorted_heads, sorted_heads)
    contributors = np.full((H, int(position.max()) + 1), head_slots * device_total, np.int32)
    contributors[sorted_heads, position] = sorted_rows
    return (head_for, source_for, item_heads, slot_heads, contributors)


def spread_rows(features, targets):
    shard_rows = features.shape[0]
    per_head = jnp.transpose(features.reshape(shard_rows, H, E), (1, 0, 2))
    padded = jnp.concatenate([per_head, jnp.zeros((1, shard_rows, E), features.dtype)], axis=0)
    return jnp.take(padded, targets, axis=0).reshape(targets.shape[0], -1)


def collect_heads(received, sources, shard_rows):
    flattened = received.reshape(-1, shard_rows * E)
    picked = jnp.take(flattened, sources, axis=0)
    return jnp.transpose(picked.reshape(H, shard_rows, E), (1, 0, 2)).reshape(shard_rows, H * E)


def place_items(pieces, segment_ids, slot_total, segments):
    per_source = pieces[0].shape[0]
    buffer = jnp.zeros((slot_total, per_source, segments, pieces[0][0].size), jnp.bfloat16)
    anchor = jnp.zeros((), jnp.int32)
    for within in range(len(pieces)):
        update = pieces[within].reshape(1, per_source, 1, -1)
        slot_start = jnp.full((), within // segments, jnp.int32)
        buffer = lax.dynamic_update_slice(
            buffer, update, (slot_start, anchor, segment_ids[within], anchor)
        )
    return buffer.reshape(slot_total, per_source * segments, -1)


def segmented(
    qkv, output_gradient, adapter_down_weight, adapter_up_weight, listed_key_blocks, key_block_count
):
    device_total = lax.axis_size("seq")
    my_index = lax.axis_index("seq")
    shard_rows = qkv.shape[0]
    segments = ITEMS_DEV * device_total // H
    slot_total = -(-ITEMS_DEV // segments)
    per_source = device_total // segments
    blocks_per_shard = shard_rows // BLOCK
    block_total = device_total * blocks_per_shard
    head_for, source_for, item_heads, slot_heads, contributors = tables(device_total, segments)
    head_slots = slot_heads.shape[1]
    residue = my_index % segments
    targets = lax.dynamic_index_in_dim(jnp.asarray(head_for), residue, 0, False)
    sources = lax.dynamic_index_in_dim(jnp.asarray(source_for), residue, 0, False)
    query_send = spread_rows(qkv[:, : H * E], targets)
    key_part = qkv[:, H * E : 2 * H * E].reshape(shard_rows, H, E)
    value_part = qkv[:, 2 * H * E :].reshape(shard_rows, H, E)
    keyval_heads = jnp.transpose(
        jnp.concatenate([key_part, value_part], axis=2), (1, 0, 2)
    ).reshape(H, shard_rows * 2 * E)
    first_head = my_index * ITEMS_DEV // segments
    received_queries, received_keyval = (
        lax.all_to_all(query_send, "seq", split_axis=0, concat_axis=0, tiled=True),
        lax.all_to_all(
            jnp.take(keyval_heads, jnp.asarray(item_heads), axis=0),
            "seq",
            split_axis=0,
            concat_axis=0,
            tiled=True,
        ),
    )
    queries_by_source = received_queries.reshape(per_source, segments, slot_total, shard_rows, E)
    keyval_by_slot = received_keyval.reshape(device_total, -1, shard_rows * 2 * E)
    source_ids = jnp.arange(per_source, dtype=jnp.int32)
    column_block = jnp.arange(KB * BLOCK, dtype=jnp.int32) // BLOCK
    saved = []
    for within in range(ITEMS_DEV):
        item_id = my_index * ITEMS_DEV + within
        item_head = item_id // segments
        segment = item_id % segments
        queries = lax.dynamic_index_in_dim(queries_by_source, segment, 1, False)[
            :, within // segments
        ]
        query_ids = (
            (segment + segments * source_ids)[:, None] * blocks_per_shard
            + jnp.arange(blocks_per_shard, dtype=jnp.int32)[None, :]
        ).reshape(-1)
        item_blocks = jnp.take(
            lax.dynamic_index_in_dim(listed_key_blocks, item_head, 0, False), query_ids, axis=0
        )
        keyval_item = lax.dynamic_index_in_dim(keyval_by_slot, within, 1, False).reshape(
            block_total, BLOCK, 2 * E
        )
        gathered = jnp.take(keyval_item, item_blocks, axis=0).reshape(-1, KB * BLOCK, 2 * E)
        live_cols = column_block < key_block_count[item_head]
        raw_scores = jnp.einsum(
            "qre,qke->qrk", queries, gathered[..., :E], preferred_element_type=jnp.float32
        ) * E ** (-0.5)
        scores = jnp.where(live_cols, raw_scores, -jnp.inf)
        row_peak = jnp.max(scores, axis=-1, keepdims=True)
        log_total = row_peak + jnp.log(jnp.sum(jnp.exp(scores - row_peak), axis=-1, keepdims=True))
        weights = jnp.exp(scores - log_total).astype(jnp.bfloat16)
        attention_output = jnp.einsum(
            "qrk,qke->qre", weights, gathered[..., E:], preferred_element_type=jnp.float32
        ).astype(jnp.bfloat16)
        saved.append(
            (item_head, segment, queries, gathered, item_blocks, weights, attention_output)
        )
    segment_ids = [entry[1] for entry in saved]
    attended_send = place_items([entry[6] for entry in saved], segment_ids, slot_total, segments)
    attended_back = lax.all_to_all(attended_send, "seq", split_axis=1, concat_axis=1, tiled=True)
    attention_output_rows = collect_heads(attended_back, sources, shard_rows)
    adapter_projected = jnp.dot(
        attention_output_rows, adapter_down_weight, preferred_element_type=jnp.float32
    ).astype(jnp.bfloat16)
    fetched_rows = jnp.einsum(
        "ec,sc->es", output_gradient, adapter_up_weight, preferred_element_type=jnp.float32
    ).astype(jnp.bfloat16)
    attention_output_gradient = (
        output_gradient.astype(jnp.float32)
        + jnp.einsum(
            "ab,eb->ae", fetched_rows, adapter_down_weight, preferred_element_type=jnp.float32
        )
    ).astype(jnp.bfloat16)
    cotangent_in = lax.all_to_all(
        spread_rows(attention_output_gradient, targets),
        "seq",
        split_axis=0,
        concat_axis=0,
        tiled=True,
    )
    down_term = jnp.einsum(
        "td,tr->dr", attention_output_rows, fetched_rows, preferred_element_type=jnp.float32
    )
    up_term = jnp.einsum(
        "tr,td->rd", adapter_projected, output_gradient, preferred_element_type=jnp.float32
    )
    grad_down, grad_up = lax.psum((down_term, up_term), "seq")
    rescale = (shard_rows * device_total) ** (-0.5)
    cotangent_by_source = cotangent_in.reshape(per_source, segments, slot_total, shard_rows, E)
    key_sums = jnp.zeros((head_slots, block_total, BLOCK, E), jnp.float32)
    value_sums = jnp.zeros((head_slots, block_total, BLOCK, E), jnp.float32)
    query_pieces = []
    for within in range(ITEMS_DEV):
        item_head, segment, queries, gathered, item_blocks, weights, attention_output = saved[
            within
        ]
        grad_item = lax.dynamic_index_in_dim(cotangent_by_source, segment, 1, False)[
            :, within // segments
        ]
        value_grad = jnp.einsum(
            "qrk,qre->qke", weights, grad_item, preferred_element_type=jnp.float32
        )
        dotted = jnp.einsum(
            "qre,qke->qrk", grad_item, gathered[..., E:], preferred_element_type=jnp.float32
        ).astype(jnp.bfloat16)
        row_delta = jnp.sum(
            grad_item.astype(jnp.float32) * attention_output.astype(jnp.float32),
            axis=-1,
            keepdims=True,
        )
        score_grad = (
            weights.astype(jnp.float32) * (dotted.astype(jnp.float32) - row_delta)
        ).astype(jnp.bfloat16)
        query_grad = (
            jnp.einsum(
                "qrk,qke->qre", score_grad, gathered[..., :E], preferred_element_type=jnp.float32
            )
            * E ** (-0.5)
        ).astype(jnp.bfloat16)
        key_grad = jnp.einsum(
            "qrk,qre->qke", score_grad, queries, preferred_element_type=jnp.float32
        ) * E ** (-0.5)
        slot_now = item_head - first_head
        key_sums = key_sums.at[slot_now, item_blocks].add(key_grad.reshape(-1, KB, BLOCK, E))
        value_sums = value_sums.at[slot_now, item_blocks].add(value_grad.reshape(-1, KB, BLOCK, E))
        query_pieces.append(query_grad)
    query_send_back = place_items(query_pieces, segment_ids, slot_total, segments)
    keyval_send_back = (
        jnp.concatenate([key_sums, value_sums], axis=-1)
        .astype(jnp.bfloat16)
        .reshape(head_slots, device_total, shard_rows * 2 * E)
    )
    query_back, keyval_back = (
        lax.all_to_all(query_send_back, "seq", split_axis=1, concat_axis=1, tiled=True),
        lax.all_to_all(keyval_send_back, "seq", split_axis=1, concat_axis=1, tiled=True),
    )
    query_rows = collect_heads(query_back, sources, shard_rows)
    stacked = jnp.concatenate(
        [
            keyval_back.reshape(head_slots * device_total, shard_rows * 2 * E),
            jnp.zeros((1, shard_rows * 2 * E), jnp.bfloat16),
        ],
        axis=0,
    )
    summed = jnp.sum(
        jnp.take(stacked, jnp.asarray(contributors), axis=0), axis=1, dtype=jnp.float32
    ).astype(jnp.bfloat16)
    keyval_rows = jnp.transpose(summed.reshape(H, shard_rows, 2 * E), (1, 0, 2))
    key_rows = keyval_rows[..., :E].reshape(shard_rows, H * E)
    value_rows = keyval_rows[..., E:].reshape(shard_rows, H * E)
    grad_qkv = jnp.concatenate([query_rows, key_rows, value_rows], axis=1)
    return (grad_qkv, grad_down * rescale, grad_up * rescale)


LOG2E = 1.4426950408889634
ROLL = E


def low_lanes(rows):
    return lax.broadcasted_iota(jnp.int32, (rows, 2 * E), 1) < E


def swap(tile):
    return pltpu.roll(tile, ROLL, 1)


def pack_kernel(qkv_ref, grad_ref, up_ref, *send_refs):
    low = low_lanes(BLOCK)
    for pair in range(H // 2):
        at = pair * 2 * E
        query, key, value = (
            qkv_ref[:, part * H * E + at : part * H * E + at + 2 * E].astype(jnp.float32)
            for part in range(3)
        )
        grad = grad_ref[:, at : at + 2 * E].astype(jnp.float32)
        for left, right, half in ((grad, query, 0), (value, key, 1)):
            lanes = slice(half * 2 * E, half * 2 * E + 2 * E)
            for head, tile in (
                (2 * pair, jnp.where(low, left, swap(right))),
                (2 * pair + 1, jnp.where(low, swap(left), right)),
            ):
                send_refs[head % ITEMS_DEV][head // ITEMS_DEV, :BLOCK, lanes] = tile.astype(
                    jnp.bfloat16
                )
    pulled = lax.dot_general(
        grad_ref[...], up_ref[...], (((1,), (1,)), ((), ())), preferred_element_type=jnp.float32
    )
    folded = jnp.concatenate(
        [pulled[part * BLOCK // 4 : (part + 1) * BLOCK // 4] for part in range(4)], axis=1
    ).astype(jnp.bfloat16)
    for device in range(send_refs[0].shape[0]):
        send_refs[0][device, BLOCK:, :] = folded


def head_kernel(forward, backward, unfold, *refs):
    refs = list(refs)
    lists_ref, counts_ref, packed_ref, wide_ref, down_ref = refs[:5]
    del refs[:5]
    block_total = packed_ref.shape[0]
    pulled_in = None if unfold else refs.pop(0)
    lowrank_in = refs.pop(0) if forward and not unfold else None
    if backward:
        rows_ref, sums = refs.pop(0), refs.pop(0)
    if unfold:
        pulled_ref = refs.pop(0)
    else:
        pulled_ref = pulled_in
    if forward:
        grad_down_ref, lowrank_ref = refs.pop(0), refs.pop(0)
    adapted, flipped, flipped_keyval, gathered, gathered_flip, attended = refs
    low = low_lanes(BLOCK)
    top = lax.broadcasted_iota(jnp.int32, (2 * E, BLOCK), 0) < E
    live = counts_ref[0]
    zero = jnp.zeros((BLOCK, 2 * E), jnp.bfloat16)

    def prepare(block, carry):
        rows = pl.ds(pl.multiple_of(block * BLOCK, BLOCK), BLOCK)
        if unfold:
            folded = packed_ref[block, BLOCK:, :]
            pulled_ref[rows, :] = jnp.concatenate(
                [folded[:, part * E : (part + 1) * E] for part in range(4)], axis=0
            )
        grad_query = packed_ref[block, :BLOCK, : 2 * E].astype(jnp.float32)
        extra = jnp.dot(pulled_ref[rows, :], wide_ref[...], preferred_element_type=jnp.float32)
        full = (grad_query + extra).astype(jnp.bfloat16)
        adapted[block] = full
        flipped[block] = full.astype(jnp.float32).T.astype(jnp.bfloat16)
        flipped_keyval[block] = (
            packed_ref[block, :BLOCK, 2 * E :].astype(jnp.float32).T.astype(jnp.bfloat16)
        )
        if backward:
            sums[block] = jnp.zeros((BLOCK, 2 * E), jnp.float32)
        return carry

    lax.fori_loop(0, block_total, prepare, 0)

    def attend(step, carry):
        blocks = [2 * step, 2 * step + 1]
        for side, block in enumerate(blocks):
            for slot in range(KB):
                listed = lists_ref[block, slot]
                span = slice(slot * BLOCK, (slot + 1) * BLOCK)
                gathered[side, span, :] = packed_ref[listed, :BLOCK, 2 * E :]
                gathered_flip[side, :, span] = flipped_keyval[listed]
        turned = [flipped[block] for block in blocks]
        both = []
        for side in range(2):
            pair = jnp.concatenate(
                [jnp.where(top, turned[side], zero), jnp.where(top, zero, turned[side])], axis=1
            )
            both.append(jnp.dot(gathered[side], pair, preferred_element_type=jnp.float32))
        slots = lax.broadcasted_iota(jnp.int32, (KB * BLOCK, BLOCK), 0)
        weights = []
        for side in range(2):
            scores = jnp.where(slots < live * BLOCK, both[side][:, BLOCK:], -jnp.inf)
            peak = jnp.max(scores, axis=0, keepdims=True)
            raised = jnp.exp2((scores - peak) * (LOG2E * E**-0.5))
            weights.append(
                (raised * (1.0 / jnp.sum(raised, axis=0, keepdims=True))).astype(jnp.bfloat16)
            )
        outputs = [
            jnp.dot(
                gathered_flip[side, :E, :], weights[side], preferred_element_type=jnp.float32
            ).astype(jnp.bfloat16)
            for side in range(2)
        ]
        if forward:
            cols = pl.ds(pl.multiple_of(step * 2 * BLOCK, 2 * BLOCK), 2 * BLOCK)
            attended[:, cols] = jnp.concatenate(outputs, axis=1)
        if not backward:
            return carry
        score_grads = []
        for side in range(2):
            delta = jnp.sum(
                outputs[side].astype(jnp.float32) * turned[side][:E].astype(jnp.float32),
                axis=0,
                keepdims=True,
            )
            score_grads.append(
                (weights[side].astype(jnp.float32) * (both[side][:, :BLOCK] - delta)).astype(
                    jnp.bfloat16
                )
            )
        partials = []
        for side, block in enumerate(blocks):
            query_grad = (
                jnp.dot(
                    gathered_flip[side, E:, :],
                    score_grads[side],
                    preferred_element_type=jnp.float32,
                )
                * E**-0.5
            )
            rows_ref[block] = jnp.concatenate(
                [query_grad, jnp.zeros_like(query_grad)], axis=0
            ).T.astype(jnp.bfloat16)
            mixed = adapted[block]
            stacked = jnp.concatenate(
                [jnp.where(low, mixed, zero), jnp.where(low, zero, mixed)], axis=0
            )
            partials.append(
                jnp.dot(
                    jnp.concatenate([weights[side], score_grads[side]], axis=1),
                    stacked,
                    preferred_element_type=jnp.float32,
                )
            )
        for side, block in enumerate(blocks):
            for slot in range(KB):
                listed = lists_ref[block, slot]
                sums[listed] += partials[side][slot * BLOCK : (slot + 1) * BLOCK]
        return carry

    lax.fori_loop(0, block_total // 2, attend, 0)

    if backward:
        def finish(block, carry):
            rows_ref[block] = jnp.where(
                low, rows_ref[block].astype(jnp.float32), sums[block] * E**-0.5
            ).astype(jnp.bfloat16)
            return carry

        lax.fori_loop(0, block_total, finish, 0)
    if forward:
        grad_down_ref[...] = jnp.dot(
            attended[...], pulled_ref[...], preferred_element_type=jnp.float32
        ) * (block_total * BLOCK) ** (-0.5)
        term = lax.dot_general(
            down_ref[...], attended[...], (((0,), (0,)), ((), ())),
            preferred_element_type=jnp.float32,
        )
        lowrank_ref[...] = term if unfold else term + lowrank_in[...]


def head_pass(forward, backward, unfold, lists, counts, packed, wide, down, *extra):
    blocks = packed.shape[0]
    rank = down.shape[-1]
    tokens = blocks * BLOCK
    vmem = pl.BlockSpec(memory_space=pltpu.VMEM)
    smem = pl.BlockSpec(memory_space=pltpu.SMEM)
    outs = []
    if backward:
        outs.append(jax.ShapeDtypeStruct((blocks, BLOCK, 2 * E), jnp.bfloat16))
        outs.append(jax.ShapeDtypeStruct((blocks, BLOCK, 2 * E), jnp.float32))
    if unfold:
        outs.append(jax.ShapeDtypeStruct((tokens, rank), jnp.bfloat16))
    if forward:
        outs.append(jax.ShapeDtypeStruct((E, rank), jnp.float32))
        outs.append(jax.ShapeDtypeStruct((rank, tokens), jnp.float32))
    return pl.pallas_call(
        functools.partial(head_kernel, forward, backward, unfold),
        out_shape=outs,
        in_specs=[smem, smem] + [vmem] * (3 + len(extra)),
        out_specs=[vmem] * len(outs),
        scratch_shapes=[
            pltpu.VMEM((blocks, BLOCK, 2 * E), jnp.bfloat16),
            pltpu.VMEM((blocks, 2 * E, BLOCK), jnp.bfloat16),
            pltpu.VMEM((blocks, 2 * E, BLOCK), jnp.bfloat16),
            pltpu.VMEM((2, KB * BLOCK, 2 * E), jnp.bfloat16),
            pltpu.VMEM((2, 2 * E, KB * BLOCK), jnp.bfloat16),
            pltpu.VMEM((E, tokens), jnp.bfloat16),
        ],
        compiler_params=pltpu.CompilerParams(vmem_limit_bytes=40 * 1024 * 1024),
        cost_estimate=pl.CostEstimate(
            flops=(20 if backward else 8) * 10**9, bytes_accessed=4 * 10**6, transcendentals=0
        ),
    )(lists, counts, packed, wide, down, *extra)


def rank_kernel(
    spread_ref, first_ref, second_ref, third_ref, out_ref,
    landed, mine, whole, send_part, recv_part, send_sum, recv_sum,
):
    count = spread_ref.shape[0]
    me = lax.axis_index("seq")

    def peer(step):
        return lax.rem(me + step, count)

    barrier = pltpu.get_barrier_semaphore()
    for step in range(1, count):
        pl.semaphore_signal(
            barrier, inc=1, device_id={"seq": peer(step)}, device_id_type=pl.DeviceIdType.MESH
        )
    pl.semaphore_wait(barrier, count - 1)

    def copy(source, target, sends, receives, step):
        return pltpu.make_async_remote_copy(
            src_ref=source,
            dst_ref=target.at[step - 1],
            send_sem=sends.at[step - 1],
            recv_sem=receives.at[step - 1],
            device_id={"seq": peer(step)},
            device_id_type=pl.DeviceIdType.MESH,
        )

    parts = [
        copy(spread_ref.at[peer(step)], landed, send_part, recv_part, step)
        for step in range(1, count)
    ]
    for part in parts:
        part.start()
    total = spread_ref[me].astype(jnp.float32)
    for step in range(1, count):
        parts[step - 1].wait_recv()
        total += landed[step - 1].astype(jnp.float32)
    mine[...] = total.astype(jnp.bfloat16)
    totals = [copy(mine, whole, send_sum, recv_sum, step) for step in range(1, count)]
    for each in totals:
        each.start()
    packed_refs = (first_ref, second_ref, third_ref)
    grads = [
        jnp.dot(mine[...], ref[me, :BLOCK, : 2 * E], preferred_element_type=jnp.float32)
        for ref in packed_refs
    ]
    for step in range(1, count):
        totals[step - 1].wait_recv()
        source = lax.rem(me + count - step, count)
        for within, ref in enumerate(packed_refs):
            grads[within] += jnp.dot(
                whole[step - 1],
                ref[source, :BLOCK, : 2 * E],
                preferred_element_type=jnp.float32,
            )
    for within in range(ITEMS_DEV):
        out_ref[within] = grads[within] * (count * BLOCK) ** (-0.5)
    for each in parts + totals:
        each.wait_send()


def unpack_kernel(early_ref, late_ref, out_ref):
    def tile(device, which):
        if which < 3:
            return early_ref[device, which].astype(jnp.float32)
        return late_ref[device, which - 3].astype(jnp.float32)

    low = low_lanes(BLOCK)
    for pair in range(H // 2):
        at = pair * 2 * E
        left, right = (
            tile(head // ITEMS_DEV, (0, 1, 3)[head % ITEMS_DEV])
            for head in (2 * pair, 2 * pair + 1)
        )
        out_ref[:, at : at + 2 * E] = jnp.where(low, left, swap(right)).astype(jnp.bfloat16)
        out_ref[:, H * E + at : H * E + at + 2 * E] = jnp.where(low, swap(left), right).astype(
            jnp.bfloat16
        )
        placed = []
        for want in range(2):
            head = 2 * pair + want
            device, within = head // ITEMS_DEV, head % ITEMS_DEV
            value = tile(device, 2 if within < 2 else 4)
            placed.append(value if within % 2 == want else swap(value))
        out_ref[:, 2 * H * E + at : 2 * H * E + at + 2 * E] = jnp.where(
            low, placed[0], placed[1]
        ).astype(jnp.bfloat16)


def whole_heads(
    qkv, output_gradient, adapter_down_weight, adapter_up_weight, listed_key_blocks, key_block_count
):
    device_total = lax.axis_size("seq")
    me = lax.axis_index("seq")
    rank = adapter_up_weight.shape[0]
    vmem = pl.BlockSpec(memory_space=pltpu.VMEM)
    params = pltpu.CompilerParams(vmem_limit_bytes=40 * 1024 * 1024)

    def exchange(array):
        return lax.all_to_all(array, "seq", 0, 0, tiled=True)

    sends = pl.pallas_call(
        pack_kernel,
        out_shape=[
            jax.ShapeDtypeStruct(
                (device_total, BLOCK + (BLOCK // 4 if within == 0 else 0), 4 * E), jnp.bfloat16
            )
            for within in range(ITEMS_DEV)
        ],
        in_specs=[vmem] * 3,
        out_specs=[vmem] * ITEMS_DEV,
        compiler_params=params,
    )(qkv, output_gradient, adapter_up_weight)
    packed0 = exchange(sends[0])
    first = me * ITEMS_DEV
    lists = lax.dynamic_slice_in_dim(listed_key_blocks, first, ITEMS_DEV, 0)
    counts = lax.dynamic_slice_in_dim(key_block_count, first, ITEMS_DEV, 0)
    down = lax.dynamic_slice_in_dim(adapter_down_weight, first * E, ITEMS_DEV * E, 0).reshape(
        ITEMS_DEV, E, rank
    )
    wide = jnp.pad(jnp.swapaxes(down, 1, 2), ((0, 0), (0, 0), (0, E)))
    def own(within, packed):
        return (
            lists[within], counts[within : within + 1], packed, wide[within], down[within]
        )

    packed0, send1 = lax.optimization_barrier((packed0, sends[1]))
    packed1 = exchange(send1)
    rows0, sums0, pulled, down0, lowrank = head_pass(True, True, True, *own(0, packed0))
    packed1, rows0, pulled, lowrank, send2 = lax.optimization_barrier(
        (packed1, rows0, pulled, lowrank, sends[2])
    )
    packed2 = exchange(send2)
    rows1, sums1, down1, lowrank = head_pass(
        True, True, False, *own(1, packed1), pulled, lowrank
    )
    values = jnp.concatenate([sums0[..., :E], sums1[..., :E]], axis=-1).astype(jnp.bfloat16)
    early = jnp.stack([rows0, rows1, values], axis=1)
    early, packed2 = lax.optimization_barrier((early, packed2))
    back1 = exchange(early)
    down2, lowrank = head_pass(True, False, False, *own(2, packed2), pulled, lowrank)
    rows2, sums2 = head_pass(False, True, False, *own(2, packed2), pulled)
    spread = jnp.swapaxes(
        lowrank.astype(jnp.bfloat16).reshape(rank, device_total, BLOCK), 0, 1
    )
    late = jnp.stack([rows2, sums2.astype(jnp.bfloat16)], axis=1)
    spread, late, back1 = lax.optimization_barrier((spread, late, back1))
    ups = pl.pallas_call(
        rank_kernel,
        out_shape=jax.ShapeDtypeStruct((ITEMS_DEV, rank, 2 * E), jnp.float32),
        in_specs=[vmem] * 4,
        out_specs=vmem,
        scratch_shapes=[
            pltpu.VMEM((device_total - 1, rank, BLOCK), jnp.bfloat16),
            pltpu.VMEM((rank, BLOCK), jnp.bfloat16),
            pltpu.VMEM((device_total - 1, rank, BLOCK), jnp.bfloat16),
        ]
        + [pltpu.SemaphoreType.DMA((device_total - 1,))] * 4,
        compiler_params=pltpu.CompilerParams(
            vmem_limit_bytes=40 * 1024 * 1024, collective_id=0, has_side_effects=True
        ),
    )(spread, packed0, packed1, packed2)
    late, ups = lax.optimization_barrier((late, ups))
    back2 = exchange(late)
    small = jnp.concatenate([jnp.stack([down0, down1, down2]), ups[..., :E]], axis=-1)
    small_all = lax.all_gather(small, "seq", axis=0, tiled=True)
    grad_qkv = pl.pallas_call(
        unpack_kernel,
        out_shape=jax.ShapeDtypeStruct(qkv.shape, jnp.bfloat16),
        in_specs=[vmem] * 2,
        out_specs=vmem,
        compiler_params=params,
    )(back1, back2)
    grad_down = small_all[..., :rank].reshape(H * E, rank)
    grad_up = jnp.swapaxes(small_all[..., rank:], 0, 1).reshape(rank, H * E)
    return (grad_qkv, grad_down, grad_up)


def shards(qkv, *others):
    if ITEMS_DEV * lax.axis_size("seq") == H and qkv.shape[0] == BLOCK:
        return whole_heads(qkv, *others)
    return segmented(qkv, *others)


def solution(mesh):
    return jax.shard_map(
        shards,
        mesh=mesh,
        in_specs=(P(("groups", "seq"), None), P(("groups", "seq"), None), P(), P(), P(), P()),
        out_specs=(P(("groups", "seq"), None), P("groups", None), P("groups", None)),
        check_vma=False,
    )
```
